32 devices in a mesh: chan: 8 (over z, x), tile: 4 (over y, core).
Axes of the slice: x: 2, y: 2, z: 4, core: 2. Of those that a mesh axis runs over, the one named last changes fastest.
Arguments:
- gamma_pair: bfloat16 [8, 2048, 2048], P('chan', 'tile'), may hold values from -8 to 8, as said below
- energies: float32 [8, 2048], P('chan'), may hold values from 0.5 to 4
- occupancy: int32 [8, 2048], P('chan'), may hold values from 0 to 2
- recoup: bfloat16 [8, 128, 128], replicated, may hold values from -0.5 to 0.5
- recoup_class: int32 [8, 16, 16], P('chan', 'tile'), may hold values from 0 to 7
- send_slot: int32 [8, 16, 16], P('chan', 'tile'), may hold values from 0 to 63, as said below
- recv_slot: int32 [8, 16, 16], P('chan', 'tile'), may hold values from 0 to 63, as said below
Outputs:
- flowed: float32 [8, 2048, 2048], P('chan', 'tile')
The draws below stay inside these ranges and needn't reach their ends.
Inputs may be any that keep to these rules, and one draw needn't show every extreme that they name: gamma_pair is symmetric in its last two dimensions. `send_slot`: for each channel and block b, the 64 entries of tile rows b * 4 to (b + 1) * 4 - 1 are a permutation of 0 to 63; entry q = 8 * c + s with 0 <= s < 8 sends the tile to channel c in its slot s, so each channel receives exactly 8 tiles from each block of each channel. `recv_slot`: for each channel and block b, the 64 entries of tile rows b * 4 to (b + 1) * 4 - 1 are a permutation of 0 to 63; entry q = 8 * c + s with 0 <= s < 8 names the tile received from channel c in its slot s.
All inputs are finite; a program needn't handle non-finite values.
Results may differ from the reference program's by a relative error of at most 0.002.
Values may be sent and summed in bfloat16 or wider, within the bound.
A program may use at most 128 MiB of HBM per device.

```python
import math
import jax
import jax.numpy as jnp
from jax import lax

W = 2048
TB = 128
NG = 8
NCH = 8
TR = 16
TRD = 4
TPD = 64
CAP = 8
N_CHAN = 8
N_TILE = 4


def draw_gamma_pair(key, part):
    normal_part = jax.random.normal(jax.random.fold_in(key, 3), (NCH, W, W), jnp.float32)
    symmetric = (normal_part + jnp.swapaxes(normal_part, 1, 2)) * 0.7071
    return jnp.clip(symmetric, -8.0, 8.0).astype(jnp.bfloat16)


def slot_table(key):
    scores = jax.random.randint(key, (NCH, TR // TRD, TPD), 0, 2 ** 20)
    scores = scores * TPD + jnp.arange(TPD, dtype=jnp.int32)[None, None, :]
    return jnp.argsort(scores, axis=-1).astype(jnp.int32).reshape(NCH, TR, TR)


def draw_send_slot(key, part):
    return slot_table(jax.random.fold_in(key, 11))


def draw_recv_slot(key, part):
    return slot_table(jax.random.fold_in(key, 23))


def place_ends(result, own_key, low, top_value):
    dims = result.shape
    spot = [jax.random.randint(jax.random.fold_in(own_key, axis), (), 0, dims[axis]) for axis in range(len(dims))]
    result = result.at[tuple(spot)].set(low)
    longest = dims.index(max(dims))
    spot[longest] = (spot[longest] + 1) % dims[longest]
    return result.at[tuple(spot)].set(top_value)


def levels(own_key, shape, shards, low, largest):
    loudness, own = 1.0, jax.random.fold_in(own_key, 6)
    for position, shards_of in shards:
        steps = jnp.exp(jax.random.uniform(jax.random.fold_in(own, position), (shards_of,), jnp.float32, low / len(shards), largest / len(shards)))
        loudness = loudness * jnp.repeat(steps, shape[position] // shards_of).reshape([-1 if axis == position else 1 for axis in range(len(shape))])
    return loudness


def normal_values(rng, shape, deviation, reach, held_as=jnp.bfloat16):
    result = deviation * jax.random.normal(rng, shape, jnp.float32)
    return jnp.clip(result, min=-reach, max=reach).astype(held_as)


def setup_inputs(seed: int = 0) -> dict:
    key_list = jax.random.split(jax.random.key(seed), 8)
    return {
        "gamma_pair": draw_gamma_pair(jax.random.fold_in(key_list[7], 71), 0),
        "energies": jnp.clip(jnp.exp(math.log(4.0) - 2.0794415 * jax.random.uniform(key_list[1], (NCH, W), jnp.float32) ** levels(key_list[1], (NCH, W), ((0, 8),), -0.2, 0.2)), 0.5, 4.0),
        "occupancy": place_ends(jax.random.randint(key_list[2], (NCH, W), 0, 3), jax.random.fold_in(key_list[2], 1), 0, 2).astype(jnp.int32),
        "recoup": normal_values(key_list[3], (NG, TB, TB), TB ** -0.5, 0.5),
        "recoup_class": place_ends(jax.random.randint(key_list[4], (NCH, TR, TR), 0, NG), jax.random.fold_in(key_list[4], 1), 0, NG - 1).astype(jnp.int32),
        "send_slot": draw_send_slot(jax.random.fold_in(key_list[7], 71), 0),
        "recv_slot": draw_recv_slot(jax.random.fold_in(key_list[7], 71), 0),
    }


def to_tiles(matrix):
    channels = matrix.shape[0]
    blocks = matrix.reshape(channels, N_TILE, TRD, TB, TR, TB)
    blocks = jnp.transpose(blocks, (0, 1, 2, 4, 3, 5))
    return blocks.reshape(channels, N_TILE, TPD, TB, TB)


def from_tiles(tile_set):
    channels = tile_set.shape[0]
    blocks = tile_set.reshape(channels, N_TILE, TRD, TR, TB, TB)
    blocks = jnp.transpose(blocks, (0, 1, 2, 4, 3, 5))
    return blocks.reshape(channels, W, W)


def pair_part(inputs):
    gamma_one, energy_one, occ_one = inputs
    occ_float = occ_one.astype(jnp.float32)
    upper_mask = ((occ_float[:, None] == 0.0) & (occ_float[None, :] == 2.0)).astype(jnp.float32)
    lower_mask = ((occ_float[:, None] == 2.0) & (occ_float[None, :] == 0.0)).astype(jnp.float32)
    denom = energy_one[:, None] + energy_one[None, :]
    eta_one = (gamma_one.astype(jnp.float32) * (upper_mask - lower_mask) / denom).astype(jnp.bfloat16)
    eta_scaled = eta_one * (1.0 - occ_float).astype(jnp.bfloat16)[None, :]
    ladder_half = jnp.dot(eta_scaled, gamma_one, preferred_element_type=jnp.float32)
    return eta_one, ladder_half + ladder_half.T


def cross_part(inputs):
    eta_cross, gamma_cross = inputs
    product = jnp.dot(eta_cross, gamma_cross, preferred_element_type=jnp.float32)
    return (product - product.T).astype(jnp.bfloat16)


def swap_groups(buffer):
    buffer = buffer.reshape(NCH, N_TILE, N_CHAN, CAP, TB, TB)
    buffer = jnp.transpose(buffer, (2, 1, 0, 3, 4, 5))
    return buffer.reshape(NCH, N_TILE, TPD, TB, TB)


def reference(gamma_pair, energies, occupancy, recoup, recoup_class, send_slot, recv_slot):
    eta_all, ladder = lax.map(pair_part, (gamma_pair, energies, occupancy))
    send_flat = send_slot.reshape(NCH, N_TILE, TPD)
    recv_flat = recv_slot.reshape(NCH, N_TILE, TPD)
    coeff_set = recoup[recoup_class.reshape(NCH, N_TILE, TPD)].astype(jnp.float32)

    def recouple(matrix):
        return jnp.einsum('cukab,cukbd->cukad', to_tiles(matrix).astype(jnp.float32), coeff_set).astype(jnp.bfloat16)

    def route_out(tile_set):
        sorter = jnp.argsort(send_flat, axis=-1).astype(jnp.int32)
        buffer = jnp.take_along_axis(tile_set, sorter[:, :, :, None, None], axis=2)
        buffer = swap_groups(buffer)
        return jnp.take_along_axis(buffer, recv_flat[:, :, :, None, None], axis=2)

    eta_cross = from_tiles(route_out(recouple(eta_all)))
    gamma_cross = from_tiles(route_out(recouple(gamma_pair)))
    cross_sym = lax.map(cross_part, (eta_cross, gamma_cross))
    sorter = jnp.argsort(recv_flat, axis=-1).astype(jnp.int32)
    buffer = jnp.take_along_axis(to_tiles(cross_sym), sorter[:, :, :, None, None], axis=2)
    buffer = swap_groups(buffer)
    pair_tiles = jnp.take_along_axis(buffer, send_flat[:, :, :, None, None], axis=2)
    back_tiles = jnp.einsum('cukab,cukdb->cukad', pair_tiles.astype(jnp.float32), coeff_set)
    back_full = from_tiles(back_tiles)
    step_size = float(W) ** -0.5
    return gamma_pair.astype(jnp.float32) + step_size * (ladder + back_full)
```

```python
import functools
import math

import jax
import jax.numpy as jnp
from jax import lax
from jax.experimental import pallas as pl
from jax.experimental.pallas import tpu as pltpu
from jax.sharding import PartitionSpec as P

MIB = 1024 * 1024
VMEM = pltpu.VMEM
SMEM = pltpu.SMEM


def whole(memory=VMEM):
    return pl.BlockSpec(memory_space=memory)


def sort_kernel(cols, tile, slot_ref, x_ref, out_ref):
    i = pl.program_id(0)
    for j in range(cols):
        out_ref[slot_ref[i * cols + j]] = x_ref[:, j * tile : (j + 1) * tile]


def sort_tiles(matrix, slots, tile):
    rows, width = matrix.shape
    cols = width // tile
    count = (rows // tile) * cols
    return pl.pallas_call(
        functools.partial(sort_kernel, cols, tile),
        grid=(rows // tile,),
        in_specs=[whole(SMEM), pl.BlockSpec((tile, width), lambda i: (i, 0))],
        out_specs=pl.BlockSpec((count, tile, tile), lambda i: (0, 0, 0)),
        out_shape=jax.ShapeDtypeStruct((count, tile, tile), matrix.dtype),
        compiler_params=pltpu.CompilerParams(vmem_limit_bytes=24 * MIB),
        name="sort_tiles",
    )(slots, matrix)


def ladder_kernel(block, row_count, where_ref, gamma_ref, xrow_ref, xcol_ref, out_ref, left):
    width = gamma_ref.shape[0]
    first = pl.multiple_of(where_ref[0], row_count)

    def scaled(g, a, b):
        return jnp.where(a * b < 0.0, -g.astype(jnp.float32) / jnp.abs(a - b), 0.0).astype(jnp.bfloat16)

    @pl.when(pl.program_id(0) == 0)
    def _():
        for i in range(row_count // 128):
            rows = pl.ds(first + i * 128, 128)
            left[i * 128 : (i + 1) * 128, :] = scaled(gamma_ref[rows, :], xrow_ref[rows, :], xcol_ref[...])

    cols = pl.ds(pl.multiple_of(pl.program_id(0) * block, block), block)
    right = gamma_ref[:, cols]
    total = jnp.dot(left[...], right, preferred_element_type=jnp.float32)
    eta = scaled(right, xrow_ref[...], xcol_ref[:, cols])
    total += jnp.dot(gamma_ref[pl.ds(first, row_count), :], eta, preferred_element_type=jnp.float32)
    out_ref[...] = total


def ladder_product(gamma_full, x, first, row_count):
    width = gamma_full.shape[0]
    block = 256
    return pl.pallas_call(
        functools.partial(ladder_kernel, block, row_count),
        grid=(width // block,),
        in_specs=[whole(SMEM), whole(), whole(), whole()],
        out_specs=pl.BlockSpec((row_count, block), lambda j: (0, j)),
        out_shape=jax.ShapeDtypeStruct((row_count, width), jnp.float32),
        scratch_shapes=[VMEM((row_count, width), jnp.bfloat16)],
        compiler_params=pltpu.CompilerParams(vmem_limit_bytes=48 * MIB),
        cost_estimate=pl.CostEstimate(
            flops=4 * row_count * width * width, bytes_accessed=8 * width * width, transcendentals=0
        ),
        name="ladder",
    )(first, gamma_full, x[:, None], x[None, :])


def cross_kernel(
    grid_cols, block, row_count, per_block, where_ref, recv_ref, meta_ref, raw_ref, recoup_ref, xseg_ref, xturn_ref, out_ref,
    eta_s, gamma_s,
):
    tile = recoup_ref.shape[1]
    lane = lax.broadcasted_iota(jnp.int32, (tile, 128), 1)
    slots = meta_ref.shape[0] // raw_ref.shape[0]
    first = pl.multiple_of(where_ref[0], row_count)
    tile_rows = per_block // grid_cols

    def place(n):
        b = n // per_block
        p = lax.rem(n, per_block)
        q = recv_ref[n]
        m = meta_ref[b * per_block + q]
        k = lax.rem(m, per_block)
        kind = lax.rem(m // per_block, recoup_ref.shape[0])
        source = m // (per_block * recoup_ref.shape[0])
        a_seg = source * grid_cols + b * tile_rows + k // grid_cols
        b_seg = source * grid_cols + lax.rem(k, grid_cols)
        turned = xturn_ref[a_seg // 128]
        xa = jnp.sum(jnp.where(lane == lax.rem(a_seg, 128), turned, 0.0), axis=1, keepdims=True)
        xb = xseg_ref[pl.ds(b_seg, 1), :]
        g = raw_ref[b, q]
        eta = jnp.where(xa * xb < 0.0, g.astype(jnp.float32) / (xa - xb), 0.0).astype(jnp.bfloat16)
        both = jnp.dot(jnp.concatenate([eta, g], axis=0), recoup_ref[kind], preferred_element_type=jnp.float32)
        both = both.astype(jnp.bfloat16)
        rows = pl.ds(pl.multiple_of((n // grid_cols) * tile, tile), tile)
        cols = pl.ds(pl.multiple_of(lax.rem(n, grid_cols) * tile, tile), tile)
        eta_s[rows, cols] = both[:tile]
        gamma_s[rows, cols] = both[tile:]

    def some(n, carry):
        for u in range(4):
            place(n * 4 + u)
        return carry

    lax.fori_loop(0, raw_ref.shape[0] * per_block // 4, some, 0)

    own_rows = pl.ds(first, row_count)
    me = first // row_count

    def product(jj, carry):
        cols = pl.ds(pl.multiple_of(jj * block, block), block)
        half = jnp.dot(eta_s[own_rows, :], gamma_s[:, cols], preferred_element_type=jnp.float32)
        mirror = jnp.dot(eta_s[cols, :], gamma_s[:, own_rows], preferred_element_type=jnp.float32)
        sym = (half - mirror.T).astype(jnp.bfloat16)
        for i in range(row_count // tile):
            for j in range(block // tile):
                slot = recv_ref[me * per_block + i * grid_cols + jj * (block // tile) + j]
                out_ref[slot] = sym[i * tile : (i + 1) * tile, j * tile : (j + 1) * tile]
        return carry

    lax.fori_loop(0, eta_s.shape[0] // block, product, 0)


def cross_product(raw, recoup, xseg, xturn, first, recv_all, meta, row_count):
    blocks, per_block, tile, _ = raw.shape
    width = blocks * row_count
    return pl.pallas_call(
        functools.partial(cross_kernel, width // tile, 256, row_count, per_block),
        in_specs=[whole(SMEM), whole(SMEM), whole(SMEM), whole(), whole(), whole(), whole()],
        out_specs=whole(),
        out_shape=jax.ShapeDtypeStruct((per_block, tile, tile), jnp.bfloat16),
        scratch_shapes=[VMEM((width, width), jnp.bfloat16), VMEM((width, width), jnp.bfloat16)],
        compiler_params=pltpu.CompilerParams(vmem_limit_bytes=52 * MIB),
        name="cross",
    )(first, recv_all, meta, raw, recoup, xseg, xturn)


def back_kernel(cols, step_size, slot_ref, kind_ref, tiles_ref, recoup_ref, gamma_ref, ladder_ref, out_ref):
    i = pl.program_id(0)
    tile = recoup_ref.shape[1]
    for j in range(cols):
        part = pl.ds(j * tile, tile)
        back = lax.dot_general(
            tiles_ref[slot_ref[i * cols + j]],
            recoup_ref[kind_ref[i * cols + j]],
            (((1,), (1,)), ((), ())),
            preferred_element_type=jnp.float32,
        )
        out_ref[:, part] = gamma_ref[:, part].astype(jnp.float32) + step_size * (ladder_ref[:, part] + back)


def finish(returned, recoup, gamma, ladder, slots, kinds):
    rows, width = gamma.shape
    count, tile, _ = returned.shape
    row_block = pl.BlockSpec((tile, width), lambda i: (i, 0))
    return pl.pallas_call(
        functools.partial(back_kernel, width // tile, 1.0 / math.sqrt(width)),
        grid=(rows // tile,),
        in_specs=[whole(SMEM), whole(SMEM), whole(), whole(), row_block, row_block],
        out_specs=row_block,
        out_shape=jax.ShapeDtypeStruct((rows, width), jnp.float32),
        compiler_params=pltpu.CompilerParams(vmem_limit_bytes=32 * MIB),
        name="finish",
    )(slots, kinds, returned, recoup, gamma, ladder)


def on_device(n_chan, n_tile, gamma_pair, energies, occupancy, recoup, recoup_class, send_slot, recv_slot):
    gamma = gamma_pair[0]
    row_count, width = gamma.shape
    tile = recoup.shape[1]
    tiles = (row_count // tile) * (width // tile)
    group = tiles // n_chan
    chan = lax.axis_index("chan")
    first = lax.axis_index("tile") * row_count
    send = send_slot.reshape(-1)
    recv = recv_slot.reshape(-1)
    kinds = recoup_class.reshape(-1)
    x = energies[0] * (1.0 - occupancy[0].astype(jnp.float32))

    local = jnp.arange(tiles, dtype=jnp.int32)
    hit = send[None, :] == local[:, None]
    entry = jnp.sum(jnp.where(hit, (local + tiles * kinds)[None, :], 0), axis=1)
    packed = jnp.concatenate(
        [
            lax.dynamic_slice_in_dim(x, first, row_count),
            entry.astype(jnp.float32),
            recv.astype(jnp.float32),
        ]
    )
    known = lax.all_gather(packed, ("chan", "tile"), axis=0, tiled=False).reshape(n_chan, n_tile, -1)
    x_all = known[:, :, :row_count].reshape(-1, tile)
    segments = x_all.shape[0]
    padded = jnp.pad(x_all, ((0, -segments % 128), (0, 0)))
    x_turned = jnp.swapaxes(padded.reshape(-1, 128, tile), 1, 2)
    entries = lax.dynamic_slice_in_dim(known, row_count + chan * group, group, 2).astype(jnp.int32)
    source = jnp.arange(n_chan, dtype=jnp.int32)[:, None, None]
    meta = jnp.transpose(entries + source * (tiles * recoup.shape[0]), (1, 0, 2)).reshape(-1)
    recv_all = lax.dynamic_slice_in_dim(known, chan, 1, 0)[0, :, row_count + tiles :].astype(jnp.int32).reshape(-1)
    where = first.reshape(1)

    out_tiles = sort_tiles(gamma, send, tile)
    arrived = lax.all_to_all(out_tiles, "chan", split_axis=0, concat_axis=0, tiled=True)
    raw = lax.all_gather(arrived, "tile", axis=0, tiled=False)
    gamma_full = lax.all_gather(gamma, "tile", axis=0, tiled=True)
    ladder = ladder_product(gamma_full, x, where, row_count)
    sym_tiles = cross_product(raw, recoup, padded, x_turned, where, recv_all, meta, row_count)
    returned = lax.all_to_all(sym_tiles, "chan", split_axis=0, concat_axis=0, tiled=True)
    return finish(returned, recoup, gamma, ladder, send, kinds)[None]


def solution(mesh):
    placed = (
        P("chan", "tile", None),
        P("chan", None),
        P("chan", None),
        P(),
        P("chan", "tile", None),
        P("chan", "tile", None),
        P("chan", "tile", None),
    )
    return jax.shard_map(
        functools.partial(on_device, mesh.shape["chan"], mesh.shape["tile"]),
        mesh=mesh, in_specs=placed, out_specs=P("chan", "tile", None), check_vma=False,
    )
```

```python
import functools
import math

import jax
import jax.numpy as jnp
from jax import lax
from jax.experimental import pallas as pl
from jax.experimental.pallas import tpu as pltpu
from jax.sharding import PartitionSpec as P

MIB = 1024 * 1024
VMEM = pltpu.VMEM
SMEM = pltpu.SMEM


def whole(memory=VMEM):
    return pl.BlockSpec(memory_space=memory)


def sort_kernel(cols, tile, slot_ref, x_ref, out_ref):
    i = pl.program_id(0)
    for j in range(cols):
        out_ref[slot_ref[i * cols + j]] = x_ref[:, j * tile : (j + 1) * tile]


def sort_tiles(matrix, slots, tile):
    rows, width = matrix.shape
    cols = width // tile
    count = (rows // tile) * cols
    return pl.pallas_call(
        functools.partial(sort_kernel, cols, tile),
        grid=(rows // tile,),
        in_specs=[whole(SMEM), pl.BlockSpec((tile, width), lambda i: (i, 0))],
        out_specs=pl.BlockSpec((count, tile, tile), lambda i: (0, 0, 0)),
        out_shape=jax.ShapeDtypeStruct((count, tile, tile), matrix.dtype),
        compiler_params=pltpu.CompilerParams(vmem_limit_bytes=24 * MIB),
        name="sort_tiles",
    )(slots, matrix)


def exchange_kernel(
    n_chan, block, group, sorted_ref, gamma_ref, info_ref, xrow_ref, xcol_ref, raw_ref, known_ref, ladder_ref,
    full, left, a_send, a_recv, f_send, f_recv, g_send, g_recv, l_sem,
):
    chan = lax.axis_index("chan")
    t = lax.axis_index("tile")
    near = t + 1 - 2 * lax.rem(t, 2)
    far = lax.rem(t + 2, 4)
    row_count, width = gamma_ref.shape
    half = width // 2
    steps = width // block

    barrier = pltpu.get_barrier_semaphore()
    for k in range(1, n_chan):
        pl.semaphore_signal(
            barrier, inc=1, device_id=(lax.rem(chan + k, n_chan), t), device_id_type=pl.DeviceIdType.MESH
        )
    for peer in (near, far):
        pl.semaphore_signal(barrier, inc=1, device_id=(chan, peer), device_id_type=pl.DeviceIdType.MESH)
    pl.semaphore_wait(barrier, n_chan + 1)

    def remote(src, dst, send, recv, device):
        return pltpu.make_async_remote_copy(
            src_ref=src, dst_ref=dst, send_sem=send, recv_sem=recv, device_id=device, device_id_type=pl.DeviceIdType.MESH
        )

    def tiles_of(c):
        return pl.ds(c * group, group)

    def outgoing(k):
        to = lax.rem(chan + k, n_chan)
        return (
            remote(info_ref, known_ref.at[chan, t], a_send.at[1, k], a_recv.at[1, k], (to, t)),
            remote(sorted_ref.at[tiles_of(to)], raw_ref.at[t, tiles_of(chan)], a_send.at[0, k], a_recv.at[0, k], (to, t)),
        )

    def onward(kind, k):
        source = lax.rem(chan - k + n_chan, n_chan)
        b = far if kind == 2 else t
        device = (chan, far if kind == 0 else near)
        at = raw_ref.at[b, tiles_of(source)]
        info = known_ref.at[source, b]
        return (
            remote(info, info, f_send.at[1, kind, k], f_recv.at[1, kind, k], device),
            remote(at, at, f_send.at[0, kind, k], f_recv.at[0, kind, k], device),
        )

    def each(copies, what):
        for copy in copies:
            getattr(copy, what)()

    rows = pl.ds(t * row_count, row_count)
    far_rows = pl.ds(far * row_count, row_count)
    own_half = pl.multiple_of((t // 2) * half, half)
    far_half = pl.multiple_of(half - own_half, half)
    own_cols = pl.ds(own_half, half)
    far_cols = pl.ds(far_half, half)
    over = remote(gamma_ref.at[:, own_cols], full.at[rows, own_cols], g_send.at[0], g_recv.at[0], (chan, far))
    beside = remote(gamma_ref, full.at[rows, :], g_send.at[1], g_recv.at[1], (chan, near))
    passed = remote(full.at[far_rows, far_cols], full.at[far_rows, far_cols], g_send.at[2], g_recv.at[2], (chan, near))
    mine = pltpu.make_async_copy(sorted_ref.at[tiles_of(chan)], raw_ref.at[t, tiles_of(chan)], l_sem.at[0])
    mine_info = pltpu.make_async_copy(info_ref, known_ref.at[chan, t], l_sem.at[1])

    over.start()
    beside.start()
    mine.start()
    mine_info.start()

    def send_out(k, carry):
        each(outgoing(k), "start")
        return carry

    lax.fori_loop(1, n_chan, send_out, 0)
    full[rows, :] = gamma_ref[...]
    mine.wait()
    mine_info.wait()
    each(onward(0, 0), "start")
    each(onward(1, 0), "start")

    def scaled(g, a, b):
        return jnp.where(a * b < 0.0, -g.astype(jnp.float32) / jnp.abs(a - b), 0.0).astype(jnp.bfloat16)

    for i in range(row_count // 128):
        part = slice(i * 128, (i + 1) * 128)
        own = pl.ds(pl.multiple_of(t * row_count + i * 128, 128), 128)
        left[part, :] = scaled(gamma_ref[part, :], xrow_ref[own, :], xcol_ref[...])

    over.wait_recv()
    passed.start()
    beside.wait_recv()
    passed.wait_recv()

    def turn(n, carry):
        across = pl.multiple_of(lax.rem(n, half // 256) * 256, 256)
        down = pl.multiple_of((n // (half // 256)) * 256, 256)
        piece = full[pl.ds(own_half + down, 256), pl.ds(far_half + across, 256)]
        full[pl.ds(far_half + across, 256), pl.ds(own_half + down, 256)] = piece.T
        return carry

    passed.wait_send()
    lax.fori_loop(0, (half // 256) ** 2, turn, 0)

    def ladder_block(j):
        cols = pl.ds(pl.multiple_of(j * block, block), block)
        right = full[:, cols]
        total = jnp.dot(left[...], right, preferred_element_type=jnp.float32)
        eta = scaled(right, xrow_ref[...], xcol_ref[:, cols])
        ladder_ref[:, cols] = total + jnp.dot(gamma_ref[...], eta, preferred_element_type=jnp.float32)

    def step(k, carry):
        each(outgoing(k), "wait_recv")
        each(onward(0, k), "start")
        each(onward(1, k), "start")
        each(onward(0, k - 1), "wait_recv")
        each(onward(2, k - 1), "start")

        @pl.when(k <= steps)
        def _():
            ladder_block(k - 1)

        return carry

    lax.fori_loop(1, n_chan, step, 0)
    each(onward(0, n_chan - 1), "wait_recv")
    each(onward(2, n_chan - 1), "start")

    def rest(j, carry):
        ladder_block(j)
        return carry

    lax.fori_loop(min(n_chan - 1, steps), steps, rest, 0)

    def drain(k, carry):
        each(onward(1, k), "wait_recv")
        each(onward(2, k), "wait_recv")
        for kind in range(3):
            each(onward(kind, k), "wait_send")
        return carry

    def drain_out(k, carry):
        each(outgoing(k), "wait_send")
        return carry

    lax.fori_loop(0, n_chan, drain, 0)
    lax.fori_loop(1, n_chan, drain_out, 0)
    over.wait_send()
    beside.wait_send()


def exchange(sorted_tiles, gamma, info, x, n_chan, n_tile):
    rows, width = gamma.shape
    count, tile, _ = sorted_tiles.shape
    anywhere = whole(pl.ANY)
    dma = pltpu.SemaphoreType.DMA
    return pl.pallas_call(
        functools.partial(exchange_kernel, n_chan, 256, count // n_chan),
        in_specs=[anywhere, whole(), anywhere, whole(), whole()],
        out_specs=[anywhere, anywhere, whole()],
        out_shape=[
            jax.ShapeDtypeStruct((n_tile, count, tile, tile), gamma.dtype),
            jax.ShapeDtypeStruct((n_chan, n_tile) + info.shape, info.dtype),
            jax.ShapeDtypeStruct((rows, width), jnp.float32),
        ],
        scratch_shapes=[
            VMEM((width, width), jnp.bfloat16),
            VMEM((rows, width), jnp.bfloat16),
            dma((2, n_chan)),
            dma((2, n_chan)),
            dma((2, 3, n_chan)),
            dma((2, 3, n_chan)),
            dma((3,)),
            dma((3,)),
            dma((2,)),
        ],
        compiler_params=pltpu.CompilerParams(vmem_limit_bytes=48 * MIB, collective_id=0, has_side_effects=True),
        cost_estimate=pl.CostEstimate(
            flops=4 * rows * width * width, bytes_accessed=16 * width * width, transcendentals=0
        ),
        name="exchange",
    )(sorted_tiles, gamma, info, x[:, None], x[None, :])


def cross_kernel(
    grid_cols, block, row_count, per_block, where_ref, recv_ref, meta_ref, raw_ref, recoup_ref, xseg_ref, xturn_ref, out_ref,
    eta_s, gamma_s,
):
    tile = recoup_ref.shape[1]
    lane = lax.broadcasted_iota(jnp.int32, (tile, 128), 1)
    slots = meta_ref.shape[0] // raw_ref.shape[0]
    first = pl.multiple_of(where_ref[0], row_count)
    tile_rows = per_block // grid_cols

    def place(n):
        b = n // per_block
        p = lax.rem(n, per_block)
        q = recv_ref[n]
        m = meta_ref[b * per_block + q]
        k = lax.rem(m, per_block)
        kind = lax.rem(m // per_block, recoup_ref.shape[0])
        source = m // (per_block * recoup_ref.shape[0])
        a_seg = source * grid_cols + b * tile_rows + k // grid_cols
        b_seg = source * grid_cols + lax.rem(k, grid_cols)
        turned = xturn_ref[a_seg // 128]
        xa = jnp.sum(jnp.where(lane == lax.rem(a_seg, 128), turned, 0.0), axis=1, keepdims=True)
        xb = xseg_ref[pl.ds(b_seg, 1), :]
        g = raw_ref[b, q]
        eta = jnp.where(xa * xb < 0.0, g.astype(jnp.float32) / (xa - xb), 0.0).astype(jnp.bfloat16)
        both = jnp.dot(jnp.concatenate([eta, g], axis=0), recoup_ref[kind], preferred_element_type=jnp.float32)
        both = both.astype(jnp.bfloat16)
        rows = pl.ds(pl.multiple_of((n // grid_cols) * tile, tile), tile)
        cols = pl.ds(pl.multiple_of(lax.rem(n, grid_cols) * tile, tile), tile)
        eta_s[rows, cols] = both[:tile]
        gamma_s[rows, cols] = both[tile:]

    def some(n, carry):
        for u in range(4):
            place(n * 4 + u)
        return carry

    lax.fori_loop(0, raw_ref.shape[0] * per_block // 4, some, 0)

    own_rows = pl.ds(first, row_count)
    me = first // row_count

    def product(jj, carry):
        cols = pl.ds(pl.multiple_of(jj * block, block), block)
        half = jnp.dot(eta_s[own_rows, :], gamma_s[:, cols], preferred_element_type=jnp.float32)
        mirror = jnp.dot(eta_s[cols, :], gamma_s[:, own_rows], preferred_element_type=jnp.float32)
        sym = (half - mirror.T).astype(jnp.bfloat16)
        for i in range(row_count // tile):
            for j in range(block // tile):
                slot = recv_ref[me * per_block + i * grid_cols + jj * (block // tile) + j]
                out_ref[slot] = sym[i * tile : (i + 1) * tile, j * tile : (j + 1) * tile]
        return carry

    lax.fori_loop(0, eta_s.shape[0] // block, product, 0)


def cross_product(raw, recoup, xseg, xturn, first, recv_all, meta, row_count):
    blocks, per_block, tile, _ = raw.shape
    width = blocks * row_count
    return pl.pallas_call(
        functools.partial(cross_kernel, width // tile, 256, row_count, per_block),
        in_specs=[whole(SMEM), whole(SMEM), whole(SMEM), whole(), whole(), whole(), whole()],
        out_specs=whole(),
        out_shape=jax.ShapeDtypeStruct((per_block, tile, tile), jnp.bfloat16),
        scratch_shapes=[VMEM((width, width), jnp.bfloat16), VMEM((width, width), jnp.bfloat16)],
        compiler_params=pltpu.CompilerParams(vmem_limit_bytes=52 * MIB),
        name="cross",
    )(first, recv_all, meta, raw, recoup, xseg, xturn)


def back_kernel(cols, step_size, slot_ref, kind_ref, tiles_ref, recoup_ref, gamma_ref, ladder_ref, out_ref):
    i = pl.program_id(0)
    tile = recoup_ref.shape[1]
    for j in range(cols):
        part = pl.ds(j * tile, tile)
        back = lax.dot_general(
            tiles_ref[slot_ref[i * cols + j]],
            recoup_ref[kind_ref[i * cols + j]],
            (((1,), (1,)), ((), ())),
            preferred_element_type=jnp.float32,
        )
        out_ref[:, part] = gamma_ref[:, part].astype(jnp.float32) + step_size * (ladder_ref[:, part] + back)


def finish(returned, recoup, gamma, ladder, slots, kinds):
    rows, width = gamma.shape
    count, tile, _ = returned.shape
    row_block = pl.BlockSpec((tile, width), lambda i: (i, 0))
    return pl.pallas_call(
        functools.partial(back_kernel, width // tile, 1.0 / math.sqrt(width)),
        grid=(rows // tile,),
        in_specs=[whole(SMEM), whole(SMEM), whole(), whole(), row_block, row_block],
        out_specs=row_block,
        out_shape=jax.ShapeDtypeStruct((rows, width), jnp.float32),
        compiler_params=pltpu.CompilerParams(vmem_limit_bytes=32 * MIB),
        name="finish",
    )(slots, kinds, returned, recoup, gamma, ladder)


def on_device(n_chan, n_tile, gamma_pair, energies, occupancy, recoup, recoup_class, send_slot, recv_slot):
    gamma = gamma_pair[0]
    row_count, width = gamma.shape
    tile = recoup.shape[1]
    tiles = (row_count // tile) * (width // tile)
    group = tiles // n_chan
    chan = lax.axis_index("chan")
    first = lax.axis_index("tile") * row_count
    send = send_slot.reshape(-1)
    recv = recv_slot.reshape(-1)
    kinds = recoup_class.reshape(-1)
    x = energies[0] * (1.0 - occupancy[0].astype(jnp.float32))

    local = jnp.arange(tiles, dtype=jnp.int32)
    hit = send[None, :] == local[:, None]
    entry = jnp.sum(jnp.where(hit, (local + tiles * kinds)[None, :], 0), axis=1)
    packed = jnp.concatenate(
        [
            lax.dynamic_slice_in_dim(x, first, row_count),
            entry.astype(jnp.float32),
            recv.astype(jnp.float32),
        ]
    )
    length = packed.shape[0]
    info = jnp.pad(packed, (0, -length % (8 * 128))).reshape(-1, 128)
    out_tiles = sort_tiles(gamma, send, tile)
    raw, known, ladder = exchange(out_tiles, gamma, info, x, n_chan, n_tile)
    known = known.reshape(n_chan, n_tile, -1)[:, :, :length]
    x_all = known[:, :, :row_count].reshape(-1, tile)
    segments = x_all.shape[0]
    padded = jnp.pad(x_all, ((0, -segments % 128), (0, 0)))
    x_turned = jnp.swapaxes(padded.reshape(-1, 128, tile), 1, 2)
    entries = lax.dynamic_slice_in_dim(known, row_count + chan * group, group, 2).astype(jnp.int32)
    source = jnp.arange(n_chan, dtype=jnp.int32)[:, None, None]
    meta = jnp.transpose(entries + source * (tiles * recoup.shape[0]), (1, 0, 2)).reshape(-1)
    recv_all = lax.dynamic_slice_in_dim(known, chan, 1, 0)[0, :, row_count + tiles :].astype(jnp.int32).reshape(-1)
    where = first.reshape(1)

    sym_tiles = cross_product(raw, recoup, padded, x_turned, where, recv_all, meta, row_count)
    returned = lax.all_to_all(sym_tiles, "chan", split_axis=0, concat_axis=0, tiled=True)
    return finish(returned, recoup, gamma, ladder, send, kinds)[None]


def solution(mesh):
    placed = (
        P("chan", "tile", None),
        P("chan", None),
        P("chan", None),
        P(),
        P("chan", "tile", None),
        P("chan", "tile", None),
        P("chan", "tile", None),
    )
    return jax.shard_map(
        functools.partial(on_device, mesh.shape["chan"], mesh.shape["tile"]),
        mesh=mesh, in_specs=placed, out_specs=P("chan", "tile", None), check_vma=False,
    )
```

```python
import functools
import math

import jax
import jax.numpy as jnp
from jax import lax
from jax.experimental import pallas as pl
from jax.experimental.pallas import tpu as pltpu
from jax.sharding import PartitionSpec as P

MIB = 1024 * 1024
VMEM = pltpu.VMEM
SMEM = pltpu.SMEM


def whole(memory=VMEM):
    return pl.BlockSpec(memory_space=memory)


def sort_kernel(cols, tile, slot_ref, x_ref, out_ref):
    i = pl.program_id(0)
    for j in range(cols):
        out_ref[slot_ref[i * cols + j]] = x_ref[:, j * tile : (j + 1) * tile]


def sort_tiles(matrix, slots, tile):
    rows, width = matrix.shape
    cols = width // tile
    count = (rows // tile) * cols
    return pl.pallas_call(
        functools.partial(sort_kernel, cols, tile),
        grid=(rows // tile,),
        in_specs=[whole(SMEM), pl.BlockSpec((tile, width), lambda i: (i, 0))],
        out_specs=pl.BlockSpec((count, tile, tile), lambda i: (0, 0, 0)),
        out_shape=jax.ShapeDtypeStruct((count, tile, tile), matrix.dtype),
        compiler_params=pltpu.CompilerParams(vmem_limit_bytes=24 * MIB),
        name="sort_tiles",
    )(slots, matrix)


def exchange_kernel(
    n_chan, block, group, sorted_ref, gamma_ref, info_ref, xrow_ref, xcol_ref, raw_ref, known_ref, ladder_ref,
    full, left, a_send, a_recv, f_send, f_recv, g_send, g_recv, l_sem,
):
    chan = lax.axis_index("chan")
    t = lax.axis_index("tile")
    near = t + 1 - 2 * lax.rem(t, 2)
    far = lax.rem(t + 2, 4)
    row_count, width = gamma_ref.shape
    half = width // 2
    steps = width // block

    barrier = pltpu.get_barrier_semaphore()
    for k in range(1, n_chan):
        pl.semaphore_signal(
            barrier, inc=1, device_id=(lax.rem(chan + k, n_chan), t), device_id_type=pl.DeviceIdType.MESH
        )
    for peer in (near, far):
        pl.semaphore_signal(barrier, inc=1, device_id=(chan, peer), device_id_type=pl.DeviceIdType.MESH)
    pl.semaphore_wait(barrier, n_chan + 1)

    def remote(src, dst, send, recv, device):
        return pltpu.make_async_remote_copy(
            src_ref=src, dst_ref=dst, send_sem=send, recv_sem=recv, device_id=device, device_id_type=pl.DeviceIdType.MESH
        )

    def tiles_of(c):
        return pl.ds(c * group, group)

    def outgoing(k):
        to = lax.rem(chan + k, n_chan)
        return (
            remote(info_ref, known_ref.at[chan, t], a_send.at[1, k], a_recv.at[1, k], (to, t)),
            remote(sorted_ref.at[tiles_of(to)], raw_ref.at[t, tiles_of(chan)], a_send.at[0, k], a_recv.at[0, k], (to, t)),
        )

    def onward(kind, k):
        source = lax.rem(chan - k + n_chan, n_chan)
        b = far if kind == 2 else t
        device = (chan, far if kind == 0 else near)
        at = raw_ref.at[b, tiles_of(source)]
        info = known_ref.at[source, b]
        return (
            remote(info, info, f_send.at[1, kind, k], f_recv.at[1, kind, k], device),
            remote(at, at, f_send.at[0, kind, k], f_recv.at[0, kind, k], device),
        )

    def each(copies, what):
        for copy in copies:
            getattr(copy, what)()

    rows = pl.ds(t * row_count, row_count)
    far_rows = pl.ds(far * row_count, row_count)
    own_half = pl.multiple_of((t // 2) * half, half)
    far_half = pl.multiple_of(half - own_half, half)
    own_cols = pl.ds(own_half, half)
    far_cols = pl.ds(far_half, half)
    over = remote(gamma_ref.at[:, own_cols], full.at[rows, own_cols], g_send.at[0], g_recv.at[0], (chan, far))
    beside = remote(gamma_ref, full.at[rows, :], g_send.at[1], g_recv.at[1], (chan, near))
    passed = remote(full.at[far_rows, far_cols], full.at[far_rows, far_cols], g_send.at[2], g_recv.at[2], (chan, near))
    mine = pltpu.make_async_copy(sorted_ref.at[tiles_of(chan)], raw_ref.at[t, tiles_of(chan)], l_sem.at[0])
    mine_info = pltpu.make_async_copy(info_ref, known_ref.at[chan, t], l_sem.at[1])

    over.start()
    beside.start()
    mine.start()
    mine_info.start()

    def send_out(k, carry):
        each(outgoing(k), "start")
        return carry

    lax.fori_loop(1, n_chan, send_out, 0)
    full[rows, :] = gamma_ref[...]
    mine.wait()
    mine_info.wait()
    each(onward(0, 0), "start")
    each(onward(1, 0), "start")

    def scaled(g, a, b):
        return jnp.where(a * b < 0.0, -g.astype(jnp.float32) / jnp.abs(a - b), 0.0).astype(jnp.bfloat16)

    for i in range(row_count // 128):
        part = slice(i * 128, (i + 1) * 128)
        own = pl.ds(pl.multiple_of(t * row_count + i * 128, 128), 128)
        left[part, :] = scaled(gamma_ref[part, :], xrow_ref[own, :], xcol_ref[...])

    def forward(k, carry):
        each(outgoing(k), "wait_recv")
        each(onward(0, k), "start")
        each(onward(1, k), "start")
        each(onward(0, k - 1), "wait_recv")
        each(onward(2, k - 1), "start")
        return carry

    early = n_chan // 2
    lax.fori_loop(1, early, forward, 0)
    over.wait_recv()
    passed.start()
    beside.wait_recv()
    passed.wait_recv()

    def turn(n, carry):
        across = pl.multiple_of(lax.rem(n, half // 256) * 256, 256)
        down = pl.multiple_of((n // (half // 256)) * 256, 256)
        piece = full[pl.ds(own_half + down, 256), pl.ds(far_half + across, 256)]
        full[pl.ds(far_half + across, 256), pl.ds(own_half + down, 256)] = piece.T
        return carry

    passed.wait_send()
    lax.fori_loop(0, (half // 256) ** 2, turn, 0)

    def ladder_block(j):
        cols = pl.ds(pl.multiple_of(j * block, block), block)
        right = full[:, cols]
        total = jnp.dot(left[...], right, preferred_element_type=jnp.float32)
        eta = scaled(right, xrow_ref[...], xcol_ref[:, cols])
        ladder_ref[:, cols] = total + jnp.dot(gamma_ref[...], eta, preferred_element_type=jnp.float32)

    def step(k, carry):
        forward(k, 0)

        @pl.when(k < early + steps)
        def _():
            ladder_block(k - early)

        return carry

    lax.fori_loop(early, n_chan, step, 0)

    def rest(j, carry):
        ladder_block(j)
        return carry

    lax.fori_loop(min(n_chan - early, steps), steps, rest, 0)
    each(onward(0, n_chan - 1), "wait_recv")
    each(onward(2, n_chan - 1), "start")

    def drain(k, carry):
        each(onward(1, k), "wait_recv")
        each(onward(2, k), "wait_recv")
        for kind in range(3):
            each(onward(kind, k), "wait_send")
        return carry

    def drain_out(k, carry):
        each(outgoing(k), "wait_send")
        return carry

    lax.fori_loop(0, n_chan, drain, 0)
    lax.fori_loop(1, n_chan, drain_out, 0)
    over.wait_send()
    beside.wait_send()


def exchange(sorted_tiles, gamma, info, x, n_chan, n_tile):
    rows, width = gamma.shape
    count, tile, _ = sorted_tiles.shape
    anywhere = whole(pl.ANY)
    dma = pltpu.SemaphoreType.DMA
    return pl.pallas_call(
        functools.partial(exchange_kernel, n_chan, 256, count // n_chan),
        in_specs=[anywhere, whole(), anywhere, whole(), whole()],
        out_specs=[anywhere, anywhere, whole()],
        out_shape=[
            jax.ShapeDtypeStruct((n_tile, count, tile, tile), gamma.dtype),
            jax.ShapeDtypeStruct((n_chan, n_tile) + info.shape, info.dtype),
            jax.ShapeDtypeStruct((rows, width), jnp.float32),
        ],
        scratch_shapes=[
            VMEM((width, width), jnp.bfloat16),
            VMEM((rows, width), jnp.bfloat16),
            dma((2, n_chan)),
            dma((2, n_chan)),
            dma((2, 3, n_chan)),
            dma((2, 3, n_chan)),
            dma((3,)),
            dma((3,)),
            dma((2,)),
        ],
        compiler_params=pltpu.CompilerParams(vmem_limit_bytes=48 * MIB, collective_id=0, has_side_effects=True),
        cost_estimate=pl.CostEstimate(
            flops=4 * rows * width * width, bytes_accessed=16 * width * width, transcendentals=0
        ),
        name="exchange",
    )(sorted_tiles, gamma, info, x[:, None], x[None, :])


def cross_kernel(
    grid_cols, block, row_count, per_block, where_ref, recv_ref, meta_ref, raw_ref, recoup_ref, xseg_ref, xturn_ref, out_ref,
    eta_s, gamma_s,
):
    tile = recoup_ref.shape[1]
    lane = lax.broadcasted_iota(jnp.int32, (tile, 128), 1)
    slots = meta_ref.shape[0] // raw_ref.shape[0]
    first = pl.multiple_of(where_ref[0], row_count)
    tile_rows = per_block // grid_cols

    def place(n):
        b = n // per_block
        p = lax.rem(n, per_block)
        q = recv_ref[n]
        m = meta_ref[b * per_block + q]
        k = lax.rem(m, per_block)
        kind = lax.rem(m // per_block, recoup_ref.shape[0])
        source = m // (per_block * recoup_ref.shape[0])
        a_seg = source * grid_cols + b * tile_rows + k // grid_cols
        b_seg = source * grid_cols + lax.rem(k, grid_cols)
        turned = xturn_ref[a_seg // 128]
        xa = jnp.sum(jnp.where(lane == lax.rem(a_seg, 128), turned, 0.0), axis=1, keepdims=True)
        xb = xseg_ref[pl.ds(b_seg, 1), :]
        g = raw_ref[b, q]
        eta = jnp.where(xa * xb < 0.0, g.astype(jnp.float32) / (xa - xb), 0.0).astype(jnp.bfloat16)
        both = jnp.dot(jnp.concatenate([eta, g], axis=0), recoup_ref[kind], preferred_element_type=jnp.float32)
        both = both.astype(jnp.bfloat16)
        rows = pl.ds(pl.multiple_of((n // grid_cols) * tile, tile), tile)
        cols = pl.ds(pl.multiple_of(lax.rem(n, grid_cols) * tile, tile), tile)
        eta_s[rows, cols] = both[:tile]
        gamma_s[rows, cols] = both[tile:]

    def some(n, carry):
        for u in range(8):
            place(n * 8 + u)
        return carry

    lax.fori_loop(0, raw_ref.shape[0] * per_block // 8, some, 0)

    own_rows = pl.ds(first, row_count)
    me = first // row_count

    def product(jj, carry):
        cols = pl.ds(pl.multiple_of(jj * block, block), block)
        half = jnp.dot(eta_s[own_rows, :], gamma_s[:, cols], preferred_element_type=jnp.float32)
        mirror = jnp.dot(eta_s[cols, :], gamma_s[:, own_rows], preferred_element_type=jnp.float32)
        sym = (half - mirror.T).astype(jnp.bfloat16)
        for i in range(row_count // tile):
            for j in range(block // tile):
                slot = recv_ref[me * per_block + i * grid_cols + jj * (block // tile) + j]
                out_ref[slot] = sym[i * tile : (i + 1) * tile, j * tile : (j + 1) * tile]
        return carry

    lax.fori_loop(0, eta_s.shape[0] // block, product, 0)


def cross_product(raw, recoup, xseg, xturn, first, recv_all, meta, row_count):
    blocks, per_block, tile, _ = raw.shape
    width = blocks * row_count
    return pl.pallas_call(
        functools.partial(cross_kernel, width // tile, 256, row_count, per_block),
        in_specs=[whole(SMEM), whole(SMEM), whole(SMEM), whole(), whole(), whole(), whole()],
        out_specs=whole(),
        out_shape=jax.ShapeDtypeStruct((per_block, tile, tile), jnp.bfloat16),
        scratch_shapes=[VMEM((width, width), jnp.bfloat16), VMEM((width, width), jnp.bfloat16)],
        compiler_params=pltpu.CompilerParams(vmem_limit_bytes=52 * MIB),
        name="cross",
    )(first, recv_all, meta, raw, recoup, xseg, xturn)


def back_kernel(cols, step_size, slot_ref, kind_ref, tiles_ref, recoup_ref, gamma_ref, ladder_ref, out_ref):
    i = pl.program_id(0)
    tile = recoup_ref.shape[1]
    for j in range(cols):
        part = pl.ds(j * tile, tile)
        back = lax.dot_general(
            tiles_ref[slot_ref[i * cols + j]],
            recoup_ref[kind_ref[i * cols + j]],
            (((1,), (1,)), ((), ())),
            preferred_element_type=jnp.float32,
        )
        out_ref[:, part] = gamma_ref[:, part].astype(jnp.float32) + step_size * (ladder_ref[:, part] + back)


def finish(returned, recoup, gamma, ladder, slots, kinds):
    rows, width = gamma.shape
    count, tile, _ = returned.shape
    row_block = pl.BlockSpec((tile, width), lambda i: (i, 0))
    return pl.pallas_call(
        functools.partial(back_kernel, width // tile, 1.0 / math.sqrt(width)),
        grid=(rows // tile,),
        in_specs=[whole(SMEM), whole(SMEM), whole(), whole(), row_block, row_block],
        out_specs=row_block,
        out_shape=jax.ShapeDtypeStruct((rows, width), jnp.float32),
        compiler_params=pltpu.CompilerParams(vmem_limit_bytes=32 * MIB),
        name="finish",
    )(slots, kinds, returned, recoup, gamma, ladder)


def on_device(n_chan, n_tile, gamma_pair, energies, occupancy, recoup, recoup_class, send_slot, recv_slot):
    gamma = gamma_pair[0]
    row_count, width = gamma.shape
    tile = recoup.shape[1]
    tiles = (row_count // tile) * (width // tile)
    group = tiles // n_chan
    chan = lax.axis_index("chan")
    first = lax.axis_index("tile") * row_count
    send = send_slot.reshape(-1)
    recv = recv_slot.reshape(-1)
    kinds = recoup_class.reshape(-1)
    x = energies[0] * (1.0 - occupancy[0].astype(jnp.float32))

    local = jnp.arange(tiles, dtype=jnp.int32)
    hit = send[None, :] == local[:, None]
    entry = jnp.sum(jnp.where(hit, (local + tiles * kinds)[None, :], 0), axis=1)
    packed = jnp.concatenate(
        [
            lax.dynamic_slice_in_dim(x, first, row_count),
            entry.astype(jnp.float32),
            recv.astype(jnp.float32),
        ]
    )
    length = packed.shape[0]
    info = jnp.pad(packed, (0, -length % (8 * 128))).reshape(-1, 128)
    out_tiles = sort_tiles(gamma, send, tile)
    raw, known, ladder = exchange(out_tiles, gamma, info, x, n_chan, n_tile)
    known = known.reshape(n_chan, n_tile, -1)[:, :, :length]
    x_all = known[:, :, :row_count].reshape(-1, tile)
    segments = x_all.shape[0]
    padded = jnp.pad(x_all, ((0, -segments % 128), (0, 0)))
    x_turned = jnp.swapaxes(padded.reshape(-1, 128, tile), 1, 2)
    entries = lax.dynamic_slice_in_dim(known, row_count + chan * group, group, 2).astype(jnp.int32)
    source = jnp.arange(n_chan, dtype=jnp.int32)[:, None, None]
    meta = jnp.transpose(entries + source * (tiles * recoup.shape[0]), (1, 0, 2)).reshape(-1)
    recv_all = lax.dynamic_slice_in_dim(known, chan, 1, 0)[0, :, row_count + tiles :].astype(jnp.int32).reshape(-1)
    where = first.reshape(1)

    sym_tiles = cross_product(raw, recoup, padded, x_turned, where, recv_all, meta, row_count)
    returned = lax.all_to_all(sym_tiles, "chan", split_axis=0, concat_axis=0, tiled=True)
    return finish(returned, recoup, gamma, ladder, send, kinds)[None]


def solution(mesh):
    placed = (
        P("chan", "tile", None),
        P("chan", None),
        P("chan", None),
        P(),
        P("chan", "tile", None),
        P("chan", "tile", None),
        P("chan", "tile", None),
    )
    return jax.shard_map(
        functools.partial(on_device, mesh.shape["chan"], mesh.shape["tile"]),
        mesh=mesh, in_specs=placed, out_specs=P("chan", "tile", None), check_vma=False,
    )
```

```python
import functools
import math

import jax
import jax.numpy as jnp
from jax import lax
from jax.experimental import pallas as pl
from jax.experimental.pallas import tpu as pltpu
from jax.sharding import PartitionSpec as P

MIB = 1024 * 1024
VMEM = pltpu.VMEM
SMEM = pltpu.SMEM


def whole(memory=VMEM):
    return pl.BlockSpec(memory_space=memory)


def sort_kernel(cols, tile, slot_ref, x_ref, out_ref):
    i = pl.program_id(0)
    for j in range(cols):
        out_ref[slot_ref[i * cols + j]] = x_ref[:, j * tile : (j + 1) * tile]


def sort_tiles(matrix, slots, tile):
    rows, width = matrix.shape
    cols = width // tile
    count = (rows // tile) * cols
    return pl.pallas_call(
        functools.partial(sort_kernel, cols, tile),
        grid=(rows // tile,),
        in_specs=[whole(SMEM), pl.BlockSpec((tile, width), lambda i: (i, 0))],
        out_specs=pl.BlockSpec((count, tile, tile), lambda i: (0, 0, 0)),
        out_shape=jax.ShapeDtypeStruct((count, tile, tile), matrix.dtype),
        compiler_params=pltpu.CompilerParams(vmem_limit_bytes=24 * MIB),
        name="sort_tiles",
    )(slots, matrix)


def exchange_kernel(
    n_chan, block, group, sorted_ref, gamma_ref, info_ref, xrow_ref, xcol_ref, raw_ref, known_ref, ladder_ref,
    full, left, a_send, a_recv, f_send, f_recv, g_send, g_recv, l_sem,
):
    chan = lax.axis_index("chan")
    t = lax.axis_index("tile")
    near = t + 1 - 2 * lax.rem(t, 2)
    far = lax.rem(t + 2, 4)
    row_count, width = gamma_ref.shape
    half = width // 2
    steps = width // block

    barrier = pltpu.get_barrier_semaphore()
    for k in range(1, n_chan):
        pl.semaphore_signal(
            barrier, inc=1, device_id=(lax.rem(chan + k, n_chan), t), device_id_type=pl.DeviceIdType.MESH
        )
    for peer in (near, far):
        pl.semaphore_signal(barrier, inc=1, device_id=(chan, peer), device_id_type=pl.DeviceIdType.MESH)
    pl.semaphore_wait(barrier, n_chan + 1)

    def remote(src, dst, send, recv, device):
        return pltpu.make_async_remote_copy(
            src_ref=src, dst_ref=dst, send_sem=send, recv_sem=recv, device_id=device, device_id_type=pl.DeviceIdType.MESH
        )

    def tiles_of(c):
        return pl.ds(c * group, group)

    def outgoing(k):
        to = lax.rem(chan + k, n_chan)
        return (
            remote(info_ref, known_ref.at[chan, t], a_send.at[1, k], a_recv.at[1, k], (to, t)),
            remote(sorted_ref.at[tiles_of(to)], raw_ref.at[t, tiles_of(chan)], a_send.at[0, k], a_recv.at[0, k], (to, t)),
        )

    def onward(kind, k):
        source = lax.rem(chan - k + n_chan, n_chan)
        b = far if kind == 2 else t
        device = (chan, far if kind == 0 else near)
        at = raw_ref.at[b, tiles_of(source)]
        info = known_ref.at[source, b]
        return (
            remote(info, info, f_send.at[1, kind, k], f_recv.at[1, kind, k], device),
            remote(at, at, f_send.at[0, kind, k], f_recv.at[0, kind, k], device),
        )

    def each(copies, what):
        for copy in copies:
            getattr(copy, what)()

    rows = pl.ds(t * row_count, row_count)
    far_rows = pl.ds(far * row_count, row_count)
    own_half = pl.multiple_of((t // 2) * half, half)
    far_half = pl.multiple_of(half - own_half, half)
    own_cols = pl.ds(own_half, half)
    far_cols = pl.ds(far_half, half)
    over = remote(gamma_ref.at[:, own_cols], full.at[rows, own_cols], g_send.at[0], g_recv.at[0], (chan, far))
    beside = remote(gamma_ref, full.at[rows, :], g_send.at[1], g_recv.at[1], (chan, near))
    passed = remote(full.at[far_rows, far_cols], full.at[far_rows, far_cols], g_send.at[2], g_recv.at[2], (chan, near))
    mine = pltpu.make_async_copy(sorted_ref.at[tiles_of(chan)], raw_ref.at[t, tiles_of(chan)], l_sem.at[0])
    mine_info = pltpu.make_async_copy(info_ref, known_ref.at[chan, t], l_sem.at[1])

    over.start()
    beside.start()
    mine.start()
    mine_info.start()

    def send_out(k, carry):
        each(outgoing(k), "start")
        return carry

    lax.fori_loop(1, n_chan, send_out, 0)
    full[rows, :] = gamma_ref[...]
    mine.wait()
    mine_info.wait()
    each(onward(0, 0), "start")
    each(onward(1, 0), "start")

    def scaled(g, a, b):
        return jnp.where(a * b < 0.0, -g.astype(jnp.float32) / jnp.abs(a - b), 0.0).astype(jnp.bfloat16)

    for i in range(row_count // 128):
        part = slice(i * 128, (i + 1) * 128)
        own = pl.ds(pl.multiple_of(t * row_count + i * 128, 128), 128)
        left[part, :] = scaled(gamma_ref[part, :], xrow_ref[own, :], xcol_ref[...])

    over.wait_recv()
    passed.start()
    beside.wait_recv()
    passed.wait_recv()

    def turn(n, carry):
        across = pl.multiple_of(lax.rem(n, half // 256) * 256, 256)
        down = pl.multiple_of((n // (half // 256)) * 256, 256)
        piece = full[pl.ds(own_half + down, 256), pl.ds(far_half + across, 256)]
        full[pl.ds(far_half + across, 256), pl.ds(own_half + down, 256)] = piece.T
        return carry

    passed.wait_send()
    lax.fori_loop(0, (half // 256) ** 2, turn, 0)

    def ladder_block(j):
        cols = pl.ds(pl.multiple_of(j * block, block), block)
        right = full[:, cols]
        total = jnp.dot(left[...], right, preferred_element_type=jnp.float32)
        eta = scaled(right, xrow_ref[...], xcol_ref[:, cols])
        ladder_ref[:, cols] = total + jnp.dot(gamma_ref[...], eta, preferred_element_type=jnp.float32)

    def step(k, carry):
        each(outgoing(k), "wait_recv")
        each(onward(0, k), "start")
        each(onward(1, k), "start")
        each(onward(0, k - 1), "wait_recv")
        each(onward(2, k - 1), "start")

        @pl.when(k <= steps)
        def _():
            ladder_block(k - 1)

        return carry

    lax.fori_loop(1, n_chan, step, 0)
    each(onward(0, n_chan - 1), "wait_recv")
    each(onward(2, n_chan - 1), "start")

    def rest(j, carry):
        ladder_block(j)
        return carry

    lax.fori_loop(min(n_chan - 1, steps), steps, rest, 0)

    def drain(k, carry):
        each(onward(1, k), "wait_recv")
        each(onward(2, k), "wait_recv")
        for kind in range(3):
            each(onward(kind, k), "wait_send")
        return carry

    def drain_out(k, carry):
        each(outgoing(k), "wait_send")
        return carry

    lax.fori_loop(0, n_chan, drain, 0)
    lax.fori_loop(1, n_chan, drain_out, 0)
    over.wait_send()
    beside.wait_send()


def exchange(sorted_tiles, gamma, info, x, n_chan, n_tile):
    rows, width = gamma.shape
    count, tile, _ = sorted_tiles.shape
    anywhere = whole(pl.ANY)
    dma = pltpu.SemaphoreType.DMA
    return pl.pallas_call(
        functools.partial(exchange_kernel, n_chan, 256, count // n_chan),
        in_specs=[anywhere, whole(), anywhere, whole(), whole()],
        out_specs=[anywhere, anywhere, whole()],
        out_shape=[
            jax.ShapeDtypeStruct((n_tile, count, tile, tile), gamma.dtype),
            jax.ShapeDtypeStruct((n_chan, n_tile) + info.shape, info.dtype),
            jax.ShapeDtypeStruct((rows, width), jnp.float32),
        ],
        scratch_shapes=[
            VMEM((width, width), jnp.bfloat16),
            VMEM((rows, width), jnp.bfloat16),
            dma((2, n_chan)),
            dma((2, n_chan)),
            dma((2, 3, n_chan)),
            dma((2, 3, n_chan)),
            dma((3,)),
            dma((3,)),
            dma((2,)),
        ],
        compiler_params=pltpu.CompilerParams(vmem_limit_bytes=48 * MIB, collective_id=0, has_side_effects=True),
        cost_estimate=pl.CostEstimate(
            flops=4 * rows * width * width, bytes_accessed=16 * width * width, transcendentals=0
        ),
        name="exchange",
    )(sorted_tiles, gamma, info, x[:, None], x[None, :])


def cross_kernel(
    grid_cols, block, row_count, per_block, where_ref, recv_ref, meta_ref, raw_ref, recoup_ref, xseg_ref, xturn_ref, out_ref,
    eta_s, gamma_s,
):
    tile = recoup_ref.shape[1]
    lane = lax.broadcasted_iota(jnp.int32, (tile, 128), 1)
    slots = meta_ref.shape[0] // raw_ref.shape[0]
    first = pl.multiple_of(where_ref[0], row_count)
    tile_rows = per_block // grid_cols

    def place(n):
        b = n // per_block
        p = lax.rem(n, per_block)
        q = recv_ref[n]
        m = meta_ref[b * per_block + q]
        k = lax.rem(m, per_block)
        kind = lax.rem(m // per_block, recoup_ref.shape[0])
        source = m // (per_block * recoup_ref.shape[0])
        a_seg = source * grid_cols + b * tile_rows + k // grid_cols
        b_seg = source * grid_cols + lax.rem(k, grid_cols)
        turned = xturn_ref[a_seg // 128]
        xa = jnp.sum(jnp.where(lane == lax.rem(a_seg, 128), turned, 0.0), axis=1, keepdims=True)
        xb = xseg_ref[pl.ds(b_seg, 1), :]
        g = raw_ref[b, q]
        eta = jnp.where(xa * xb < 0.0, g.astype(jnp.float32) / (xa - xb), 0.0).astype(jnp.bfloat16)
        both = jnp.dot(jnp.concatenate([eta, g], axis=0), recoup_ref[kind], preferred_element_type=jnp.float32)
        both = both.astype(jnp.bfloat16)
        rows = pl.ds(pl.multiple_of((n // grid_cols) * tile, tile), tile)
        cols = pl.ds(pl.multiple_of(lax.rem(n, grid_cols) * tile, tile), tile)
        eta_s[rows, cols] = both[:tile]
        gamma_s[rows, cols] = both[tile:]

    def some(n, carry):
        for u in range(16):
            place(n * 16 + u)
        return carry

    lax.fori_loop(0, raw_ref.shape[0] * per_block // 16, some, 0)

    own_rows = pl.ds(first, row_count)
    me = first // row_count

    def product(jj, carry):
        cols = pl.ds(pl.multiple_of(jj * block, block), block)
        half = jnp.dot(eta_s[own_rows, :], gamma_s[:, cols], preferred_element_type=jnp.float32)
        mirror = jnp.dot(eta_s[cols, :], gamma_s[:, own_rows], preferred_element_type=jnp.float32)
        sym = (half - mirror.T).astype(jnp.bfloat16)
        for i in range(row_count // tile):
            for j in range(block // tile):
                slot = recv_ref[me * per_block + i * grid_cols + jj * (block // tile) + j]
                out_ref[slot] = sym[i * tile : (i + 1) * tile, j * tile : (j + 1) * tile]
        return carry

    lax.fori_loop(0, eta_s.shape[0] // block, product, 0)


def cross_product(raw, recoup, xseg, xturn, first, recv_all, meta, row_count):
    blocks, per_block, tile, _ = raw.shape
    width = blocks * row_count
    return pl.pallas_call(
        functools.partial(cross_kernel, width // tile, 256, row_count, per_block),
        in_specs=[whole(SMEM), whole(SMEM), whole(SMEM), whole(), whole(), whole(), whole()],
        out_specs=whole(),
        out_shape=jax.ShapeDtypeStruct((per_block, tile, tile), jnp.bfloat16),
        scratch_shapes=[VMEM((width, width), jnp.bfloat16), VMEM((width, width), jnp.bfloat16)],
        compiler_params=pltpu.CompilerParams(vmem_limit_bytes=52 * MIB),
        name="cross",
    )(first, recv_all, meta, raw, recoup, xseg, xturn)


def back_kernel(cols, step_size, slot_ref, kind_ref, tiles_ref, recoup_ref, gamma_ref, ladder_ref, out_ref):
    i = pl.program_id(0)
    tile = recoup_ref.shape[1]
    for j in range(cols):
        part = pl.ds(j * tile, tile)
        back = lax.dot_general(
            tiles_ref[slot_ref[i * cols + j]],
            recoup_ref[kind_ref[i * cols + j]],
            (((1,), (1,)), ((), ())),
            preferred_element_type=jnp.float32,
        )
        out_ref[:, part] = gamma_ref[:, part].astype(jnp.float32) + step_size * (ladder_ref[:, part] + back)


def finish(returned, recoup, gamma, ladder, slots, kinds):
    rows, width = gamma.shape
    count, tile, _ = returned.shape
    row_block = pl.BlockSpec((tile, width), lambda i: (i, 0))
    return pl.pallas_call(
        functools.partial(back_kernel, width // tile, 1.0 / math.sqrt(width)),
        grid=(rows // tile,),
        in_specs=[whole(SMEM), whole(SMEM), whole(), whole(), row_block, row_block],
        out_specs=row_block,
        out_shape=jax.ShapeDtypeStruct((rows, width), jnp.float32),
        compiler_params=pltpu.CompilerParams(vmem_limit_bytes=32 * MIB),
        name="finish",
    )(slots, kinds, returned, recoup, gamma, ladder)


def on_device(n_chan, n_tile, gamma_pair, energies, occupancy, recoup, recoup_class, send_slot, recv_slot):
    gamma = gamma_pair[0]
    row_count, width = gamma.shape
    tile = recoup.shape[1]
    tiles = (row_count // tile) * (width // tile)
    group = tiles // n_chan
    chan = lax.axis_index("chan")
    first = lax.axis_index("tile") * row_count
    send = send_slot.reshape(-1)
    recv = recv_slot.reshape(-1)
    kinds = recoup_class.reshape(-1)
    x = energies[0] * (1.0 - occupancy[0].astype(jnp.float32))

    local = jnp.arange(tiles, dtype=jnp.int32)
    hit = send[None, :] == local[:, None]
    entry = jnp.sum(jnp.where(hit, (local + tiles * kinds)[None, :], 0), axis=1)
    packed = jnp.concatenate(
        [
            lax.dynamic_slice_in_dim(x, first, row_count),
            entry.astype(jnp.float32),
            recv.astype(jnp.float32),
        ]
    )
    length = packed.shape[0]
    info = jnp.pad(packed, (0, -length % (8 * 128))).reshape(-1, 128)
    out_tiles = sort_tiles(gamma, send, tile)
    raw, known, ladder = exchange(out_tiles, gamma, info, x, n_chan, n_tile)
    known = known.reshape(n_chan, n_tile, -1)[:, :, :length]
    x_all = known[:, :, :row_count].reshape(-1, tile)
    segments = x_all.shape[0]
    padded = jnp.pad(x_all, ((0, -segments % 128), (0, 0)))
    x_turned = jnp.swapaxes(padded.reshape(-1, 128, tile), 1, 2)
    entries = lax.dynamic_slice_in_dim(known, row_count + chan * group, group, 2).astype(jnp.int32)
    source = jnp.arange(n_chan, dtype=jnp.int32)[:, None, None]
    meta = jnp.transpose(entries + source * (tiles * recoup.shape[0]), (1, 0, 2)).reshape(-1)
    recv_all = lax.dynamic_slice_in_dim(known, chan, 1, 0)[0, :, row_count + tiles :].astype(jnp.int32).reshape(-1)
    where = first.reshape(1)

    sym_tiles = cross_product(raw, recoup, padded, x_turned, where, recv_all, meta, row_count)
    returned = lax.all_to_all(sym_tiles, "chan", split_axis=0, concat_axis=0, tiled=True)
    return finish(returned, recoup, gamma, ladder, send, kinds)[None]


def solution(mesh):
    placed = (
        P("chan", "tile", None),
        P("chan", None),
        P("chan", None),
        P(),
        P("chan", "tile", None),
        P("chan", "tile", None),
        P("chan", "tile", None),
    )
    return jax.shard_map(
        functools.partial(on_device, mesh.shape["chan"], mesh.shape["tile"]),
        mesh=mesh, in_specs=placed, out_specs=P("chan", "tile", None), check_vma=False,
    )
```
